32 devices in a mesh: section: 2 (over x), tm: 4 (over y, core), dp: 4 (over z).
Axes of the slice: x: 2, y: 2, z: 4, core: 2. Of those that a mesh axis runs over, the one named last changes fastest.
Arguments:
- frames: bfloat16 [8, 2048, 512], P(('section', 'dp'), 'tm'), may hold values from -6 to 6
- lengths: int32 [8], P(('section', 'dp')), may hold values from 10240 to 40960, as said below
- fourth_conv: bfloat16 [3, 512, 512], P(None, ('section', 'dp')), may hold values from -0.15625 to 0.15625
- fifth_conv: bfloat16 [3, 512, 512], P(None, ('section', 'dp')), may hold values from -0.15625 to 0.15625
- sixth_conv: bfloat16 [2, 512, 512], P(None, ('section', 'dp')), may hold values from -0.1875 to 0.1875
- seventh_conv: bfloat16 [2, 512, 512], P(None, ('section', 'dp')), may hold values from -0.1875 to 0.1875
- norm_gain: float32 [512], replicated, may hold values from 0.5 to 1.5
- norm_bias: float32 [512], replicated, may hold values from -1.8 to 1.8
- project_weight: bfloat16 [512, 480], P(None, 'tm'), may hold values from -0.25 to 0.25
- project_bias: bfloat16 [1, 480], P(None, 'tm'), may hold values from -1.796875 to 1.796875
- position_weight: bfloat16 [4, 128, 14400], P('tm', ('section', 'dp')), may hold values from -0.046875 to 0.046875
- position_bias: float32 [480], P('tm'), may hold values from -3 to 3
Outputs:
- encoded: bfloat16 [8, 480, 128], P(('section', 'dp'), 'tm')
The draws below stay inside these ranges and needn't reach their ends.
Inputs may be any that keep to these rules, and one draw needn't show every extreme that they name: `lengths`: length of each utterance in samples; some utterance of every draw fills all 2048 input frames.
All inputs are finite; a program needn't handle non-finite values.
Results may differ from the reference program's by a relative error of at most 0.012.
Values may be sent and summed in bfloat16 or wider, within the bound.
No kernel may reach another device: no remote copies, remote signals or barrier semaphores. Data moves between devices by JAX's collectives and lax.ppermute only.
A program may use at most 64 MiB of HBM per device.

```python
import jax
import jax.numpy as jnp
from jax import lax

CONV_DIM = 512
GROUP_WIDTH = 120
TAPS = 128
GROUPS = 4
HIDDEN_SIZE = 480
FRAMES = 128
IN_FRAMES = 2048
UTTERANCES = 8


def draw_lengths(key, part):
    key_one, key_two = jax.random.split(jax.random.fold_in(key, 7))
    longest = IN_FRAMES * 20
    lengths_drawn = jax.random.randint(key_one, (UTTERANCES,), IN_FRAMES * 5, longest + 1, dtype=jnp.int32)
    chosen = jax.random.randint(key_two, (), 0, UTTERANCES, dtype=jnp.int32)
    return lengths_drawn.at[chosen].set(longest)


def block_scale(key, dims, cuts, low, largest):
    def one(dim, parts):
        heights = jax.random.uniform(jax.random.fold_in(jax.random.fold_in(key, 6), dim), (parts,), jnp.float32, low / len(cuts), largest / len(cuts))
        return jnp.repeat(jnp.exp(heights), dims[dim] // parts).reshape((-1,) + (1,) * (len(dims) - dim - 1))

    level = one(*cuts[0])
    for cut in cuts[1:]:
        level = level * one(*cut)
    return level


def noise(stream_key, shape, scale, reach, cuts=(), kind=jnp.bfloat16):
    gain = block_scale(stream_key, shape, cuts, -0.22, 0.18) if cuts else 1.0
    drawn = jax.random.normal(stream_key, shape, jnp.float32) * scale * gain
    return jnp.minimum(jnp.maximum(drawn, -reach), reach).astype(kind)


def setup_inputs(seed: int = 0) -> dict:
    seeds = jax.random.split(jax.random.key(seed), 13)
    frames = noise(seeds[0], (UTTERANCES, IN_FRAMES, CONV_DIM), 1.0, 6.0, ((0, 8), (1, 4)))
    lengths = draw_lengths(jax.random.fold_in(seeds[12], 71), 0)
    fourth_conv = noise(seeds[2], (3, CONV_DIM, CONV_DIM), (3 * CONV_DIM) ** -0.5, 0.15625, ((1, 8),))
    fifth_conv = noise(seeds[3], (3, CONV_DIM, CONV_DIM), (3 * CONV_DIM) ** -0.5, 0.15625, ((1, 8),))
    sixth_conv = noise(seeds[4], (2, CONV_DIM, CONV_DIM), (2 * CONV_DIM) ** -0.5, 0.1875, ((1, 8),))
    seventh_conv = noise(seeds[5], (2, CONV_DIM, CONV_DIM), (2 * CONV_DIM) ** -0.5, 0.1875, ((1, 8),))
    norm_gain = jnp.clip(1.0 + 0.1 * jax.random.normal(seeds[6], (CONV_DIM,), jnp.float32), 0.5, 1.5)
    norm_bias = noise(seeds[7], (CONV_DIM,), 0.3, 1.8, (), jnp.float32)
    project_weight = noise(seeds[8], (CONV_DIM, HIDDEN_SIZE), CONV_DIM ** -0.5, 0.25, ((1, 4),))
    project_bias = noise(seeds[9], (1, HIDDEN_SIZE), 0.3, 1.796875, ((1, 4),))
    position_weight = noise(seeds[10], (GROUPS, TAPS, GROUP_WIDTH * GROUP_WIDTH), (TAPS * GROUP_WIDTH) ** -0.5, 0.046875, ((0, 4), (1, 8)))
    position_bias = noise(seeds[11], (HIDDEN_SIZE,), 0.5, 3.0, ((0, 4),), jnp.float32)
    return {"frames": frames, "lengths": lengths, "fourth_conv": fourth_conv, "fifth_conv": fifth_conv, "sixth_conv": sixth_conv, "seventh_conv": seventh_conv, "norm_gain": norm_gain, "norm_bias": norm_bias, "project_weight": project_weight, "project_bias": project_bias, "position_weight": position_weight, "position_bias": position_bias}


eps_norm = 1e-05

def layer_norm(values):
    average = lax.optimization_barrier(jnp.mean(values, axis=-1, keepdims=True))
    centred = values - average
    spread = lax.optimization_barrier(jnp.mean(centred * centred, axis=-1, keepdims=True))
    return centred * lax.rsqrt(spread + eps_norm)

def strided_conv(inputs, weight):
    row_count = inputs.shape[0]
    channels = inputs.shape[1]
    padded = jnp.concatenate([inputs, jnp.zeros((2, channels), inputs.dtype)], axis=0)
    paired = padded.reshape(row_count // 2 + 1, 2, channels)
    even_rows = paired[:, 0]
    odd_rows = paired[:, 1]
    out_rows = row_count // 2
    summed = jnp.dot(even_rows[:out_rows], weight[0], preferred_element_type=jnp.float32)
    summed = summed + jnp.dot(odd_rows[:out_rows], weight[1], preferred_element_type=jnp.float32)
    if weight.shape[0] == 3:
        summed = summed + jnp.dot(even_rows[1:out_rows + 1], weight[2], preferred_element_type=jnp.float32)
    return jax.nn.gelu(layer_norm(summed), approximate=False).astype(jnp.bfloat16)

def reference(frames, lengths, fourth_conv, fifth_conv, sixth_conv, seventh_conv, norm_gain, norm_bias, project_weight, project_bias, position_weight, position_bias):
    kernel = position_weight.astype(jnp.float32).reshape(GROUPS, TAPS, GROUP_WIDTH, GROUP_WIDTH)
    kernel = kernel.transpose(0, 2, 3, 1).reshape(HIDDEN_SIZE, GROUP_WIDTH, TAPS)

    def one_utterance(members):
        inputs, length = members
        sample_index = jnp.arange(IN_FRAMES, dtype=jnp.int32)
        current = jnp.where((sample_index * 20 < length)[:, None], inputs, jnp.zeros_like(inputs))
        for weight in (fourth_conv, fifth_conv, sixth_conv, seventh_conv):
            current = strided_conv(current, weight)
        normed = (layer_norm(current.astype(jnp.float32)) * norm_gain + norm_bias).astype(jnp.bfloat16)
        hidden = (jnp.dot(normed, project_weight, preferred_element_type=jnp.float32) + project_bias.astype(jnp.float32)).astype(jnp.bfloat16)
        frame_index = jnp.arange(FRAMES, dtype=jnp.int32)
        hidden = jnp.where((frame_index * 320 < length)[:, None], hidden, jnp.zeros_like(hidden))
        channels_first = hidden.astype(jnp.float32).T
        conv = lax.conv_general_dilated(channels_first[None], kernel, (1,), [(TAPS // 2, TAPS // 2 - 1)], dimension_numbers=('NCH', 'OIH', 'NCH'), feature_group_count=GROUPS, precision=lax.Precision.HIGHEST)[0]
        position = jax.nn.gelu(conv + position_bias[:, None], approximate=False)
        return (channels_first + position).astype(jnp.bfloat16)
    return lax.map(one_utterance, (frames, lengths))
```

```python
import functools

import jax
import jax.numpy as jnp
from jax import lax
from jax.experimental import pallas as pl
from jax.experimental.pallas import tpu as pltpu
from jax.sharding import PartitionSpec as P

TAPS = 128
ROW_TILE = 16
LANES = 128
PHASES = 16
SHARDED = ("section", "dp")
eps_norm = 1e-05
f32 = jnp.float32
bf16 = jnp.bfloat16


def bits_of(size):
    return [1 << b for b in range(size.bit_length() - 1)]


def swapped(x, axis, bit):
    return lax.ppermute(x, axis, [(i, i ^ bit) for i in range(lax.axis_size(axis))])


def swapped_by_parity(x, section_bit, tm_bit, section_first):
    sections, shares = lax.axis_size("section"), lax.axis_size("tm")
    pairs = []
    for s in range(sections):
        for t in range(shares):
            over_section = (t % 2 == 0) == section_first
            to = (s ^ section_bit, t) if over_section else (s, t ^ tm_bit)
            pairs.append((s * shares + t, to[0] * shares + to[1]))
    return lax.ppermute(x, ("section", "tm"), pairs)


def flipped(where, axis, bit):
    return tuple(w ^ (bit if name == axis else 0) for w, name in zip(where, ("section", "dp", "tm"), strict=True))


def gather_weights(own, parts):
    here = (0, 0, 0)
    distances = list(range(lax.axis_size("dp")))
    received = [own] + [swapped(own, "dp", k) for k in distances[1:]]
    pieces = []
    for k in range(0, len(received), 2):
        pair = received[k : k + 2]
        origins = [flipped(here, "dp", d) for d in distances[k : k + 2]]
        pieces.append((jnp.stack(pair), [(o, o) for o in origins]))
    section_bits = bits_of(lax.axis_size("section"))
    mixed = parts == 4 and section_bits
    for bit in section_bits[: -1 if mixed else None]:
        pieces += [
            (swapped(x, "section", bit), [(flipped(e, "section", bit), flipped(o, "section", bit)) for e, o in origins])
            for x, origins in pieces
        ]
    if mixed:
        bit = section_bits[-1]
        first = [
            (swapped_by_parity(x, bit, 2, True), [(flipped(e, "section", bit), flipped(o, "tm", 2)) for e, o in origins])
            for x, origins in pieces
        ]
        both = pieces + first
        second = [
            (swapped_by_parity(x, bit, 2, False), [(flipped(e, "tm", 2), flipped(o, "section", bit)) for e, o in origins])
            for x, origins in both
        ]
        pieces = both + second
    elif parts == 4:
        pieces += [
            (swapped(x, "tm", 2), [(flipped(e, "tm", 2), flipped(o, "tm", 2)) for e, o in origins]) for x, origins in pieces
        ]
    if parts >= 2:
        pieces += [
            (swapped(x, "tm", 1), [(flipped(o, "tm", 1), flipped(e, "tm", 1)) for e, o in origins]) for x, origins in pieces
        ]
    return [x for x, _ in pieces], [origin for _, origins in pieces for origin in origins]


def weight_rows(origins, parts, shard_rows):
    odd = lax.axis_index("tm") % 2
    picked = jnp.where(odd == 1, jnp.array([o for _, o in origins]), jnp.array([e for e, _ in origins]))
    section = lax.axis_index("section") ^ picked[:, 0]
    stage = lax.axis_index("dp") ^ picked[:, 1]
    part = (lax.axis_index("tm") % parts) ^ picked[:, 2]
    shard = section * lax.axis_size("dp") + stage
    return (shard * shard_rows + part * (shard_rows // parts)).astype(jnp.int32)


def layer_norm(values):
    average = jnp.mean(values, axis=-1, keepdims=True)
    centred = values - average
    spread = jnp.mean(centred * centred, axis=-1, keepdims=True)
    return centred * lax.rsqrt(spread + eps_norm)


def gelu(values):
    return 0.5 * values * (1.0 + lax.erf(values * (0.5**0.5)))


def dot(a, b):
    return jnp.dot(a, b, preferred_element_type=f32)


def dot_nt(a, b):
    return lax.dot_general(a, b, (((1,), (1,)), ((), ())), preferred_element_type=f32)


def put_rows(rows_ref, start, values):
    values = values.astype(f32)
    for block in range(rows_ref.shape[0]):
        rows_ref[block, pl.ds(start, values.shape[0]), :] = values[:, block * LANES : (block + 1) * LANES]


def strided_conv(rows_ref, weight_ref, out_rows):
    summed = None
    for tap in range(weight_ref.shape[0]):
        picked = jnp.concatenate(
            [rows_ref[block, pl.ds(tap, out_rows, stride=2), :].astype(bf16) for block in range(rows_ref.shape[0])],
            axis=1,
        )
        term = dot(picked, weight_ref[tap])
        summed = term if summed is None else summed + term
    return gelu(layer_norm(summed)).astype(bf16)


def start_assembly(piece_refs, first_rows, tap_slices, weight_refs, sems):
    for layer, (low, high) in enumerate(tap_slices):
        for index, piece in enumerate(piece_refs):
            slots, rows = piece.shape[0], piece.shape[2]
            for slot in range(slots):
                row = pl.multiple_of(first_rows[index * slots + slot], ROW_TILE)
                pltpu.make_async_copy(
                    piece.at[slot, low:high],
                    weight_refs[layer].at[:, pl.ds(row, rows), :],
                    sems.at[layer],
                ).start()


def wait_assembly(weight_ref, sem):
    pltpu.make_async_copy(weight_ref, weight_ref, sem).wait()


def front_kernel(n_pieces, tap_slices, first_rows, scalars, frames, halo, *rest):
    pieces, out = rest[:n_pieces], rest[n_pieces]
    w_a, w_b, x_in, x_mid, sems = rest[n_pieces + 1 :]
    start_assembly(pieces, first_rows, tap_slices, (w_a, w_b), sems)
    length, first = scalars[0], scalars[1]
    rows, halo_rows = frames.shape[0], halo.shape[0]
    channels = frames.shape[1]

    def masked(values, start):
        index = lax.broadcasted_iota(jnp.int32, (values.shape[0], 1), 0) + start
        return jnp.where(index * 20 < length, values.astype(f32), 0.0)

    put_rows(x_in, 0, masked(frames[...], first))
    put_rows(x_in, rows, masked(halo[...], first + rows))
    put_rows(x_in, rows + halo_rows, jnp.zeros((x_in.shape[1] - rows - halo_rows, channels), f32))
    wait_assembly(w_a, sems.at[0])
    put_rows(x_mid, 0, strided_conv(x_in, w_a, x_mid.shape[1]))
    wait_assembly(w_b, sems.at[1])
    out[...] = strided_conv(x_mid, w_b, out.shape[0])


def back_kernel(n_pieces, n_rows, tap_slices, first_rows, scalars, gain, bias, project, project_bias, *rest):
    pieces, row_pieces, out = rest[:n_pieces], rest[n_pieces : n_pieces + n_rows], rest[n_pieces + n_rows]
    w_a, w_b, x_in, x_mid, sems = rest[n_pieces + n_rows + 1 :]
    start_assembly(pieces, first_rows, tap_slices, (w_a, w_b), sems)
    length, tm = scalars[0], scalars[2]
    for index, piece in enumerate(row_pieces):
        rows = piece.shape[0]
        put_rows(x_in, pl.multiple_of((tm ^ index) * rows, ROW_TILE), piece[...])
    wait_assembly(w_a, sems.at[0])
    put_rows(x_mid, 0, strided_conv(x_in, w_a, x_mid.shape[1]))
    wait_assembly(w_b, sems.at[1])
    frames, group = out.shape[0], project.shape[0]
    extracted = strided_conv(x_mid, w_b, frames).astype(f32)
    normed = (layer_norm(extracted) * gain[...] + bias[...]).astype(bf16)
    hidden = (dot_nt(normed, project[...]) + project_bias[...].astype(f32)).astype(bf16)
    index = lax.broadcasted_iota(jnp.int32, (frames, 1), 0)
    hidden = jnp.where(index * 320 < length, hidden.astype(f32), 0.0)
    out[...] = jnp.zeros(out.shape, bf16)
    out[:, 0:group] = hidden.astype(bf16)


def position_kernel(n_pieces, offsets, hidden, *rest):
    pieces, out, padded, phases = rest[:n_pieces], rest[n_pieces], rest[n_pieces + 1], rest[n_pieces + 2]
    frames = hidden.shape[0]
    padded[...] = jnp.zeros(padded.shape, f32)
    padded[TAPS // 2 : TAPS // 2 + frames, :] = hidden[...].astype(f32)
    taps, width = pieces[0].shape[0], pieces[0].shape[1]
    span = phases.shape[0]
    for index, piece in enumerate(pieces):
        window = padded[pl.ds(offsets[index], span), :].astype(bf16)
        term = dot_nt(window, piece[...].reshape(taps * width, piece.shape[2]))
        if index == 0:
            phases[...] = term
        else:
            phases[...] += term
    total = phases[0:frames, 0:width]
    for tap in range(1, taps):
        total = total + phases[tap : tap + frames, tap * width : (tap + 1) * width]
    out[...] = total.astype(out.dtype)


def final_kernel(group, hidden, mine, theirs, bias, out):
    conv = mine[...] + theirs[...].astype(f32)
    encoded = hidden[...].astype(f32) + gelu(conv + bias[...])
    out[...] = jnp.transpose(encoded)[0:group, :].astype(bf16)


def vmem(count):
    return [pl.BlockSpec(memory_space=pltpu.VMEM)] * count


def smem(count):
    return [pl.BlockSpec(memory_space=pltpu.SMEM)] * count


def unplaced(count):
    return [pl.BlockSpec(memory_space=pl.ANY)] * count


LIMIT = pltpu.CompilerParams(vmem_limit_bytes=40 * 1024 * 1024)


def local(
    frames,
    lengths,
    fourth_conv,
    fifth_conv,
    sixth_conv,
    seventh_conv,
    norm_gain,
    norm_bias,
    project_weight,
    project_bias,
    position_weight,
    position_bias,
):
    sections, stages, shares = (lax.axis_size(a) for a in ("section", "dp", "tm"))
    section, stage, tm = (lax.axis_index(a) for a in ("section", "dp", "tm"))
    rows, channels = frames.shape[1:]
    shard_rows = fourth_conv.shape[1]
    parts = max(p for p in (1, 2, 4) if p <= shares and shard_rows % (p * ROW_TILE) == 0)
    part_rows = shard_rows // parts
    part = tm % parts

    def own_part(weights):
        return jnp.concatenate(
            [lax.dynamic_slice_in_dim(w, part * part_rows, part_rows, 1) for w in weights], axis=0
        )

    halo = lax.ppermute(frames[0, :ROW_TILE], "tm", [(i + 1, i) for i in range(shares - 1)])
    front_pieces, origins = gather_weights(own_part([fourth_conv, fifth_conv]), parts)
    back_pieces, _ = gather_weights(own_part([sixth_conv, seventh_conv]), parts)
    first_rows = weight_rows(origins, parts, shard_rows)
    scalars = jnp.stack([lengths[0], tm * rows, tm]).astype(jnp.int32)

    group = position_bias.shape[0]
    own_taps = position_weight.shape[1]
    taps = position_weight[0].reshape(own_taps, group, group)
    taps = jnp.pad(taps, ((0, 0), (0, LANES - group), (0, LANES - group)))
    tap_pieces, tap_places = [taps], [(0, 0, 0)]
    for axis, bits in (("section", bits_of(sections)), ("dp", bits_of(stages)[:-1])):
        for bit in bits:
            tap_pieces += [swapped(x, axis, bit) for x in tap_pieces]
            tap_places += [flipped(p, axis, bit) for p in tap_places]
    offsets = jnp.stack(
        [((section ^ p[0]) * stages + (stage ^ p[1])) * own_taps for p in tap_places]
    ).astype(jnp.int32)

    taps_of = [w.shape[0] for w in (fourth_conv, fifth_conv, sixth_conv, seventh_conv)]
    n_pieces = len(front_pieces)
    blocks = channels // LANES
    mid_rows = (rows // 2 + 8) // 8 * 8
    y_front = pl.pallas_call(
        functools.partial(front_kernel, n_pieces, [(0, taps_of[0]), (taps_of[0], taps_of[0] + taps_of[1])]),
        out_shape=jax.ShapeDtypeStruct((rows // 4, channels), bf16),
        in_specs=smem(2) + vmem(2) + unplaced(n_pieces),
        out_specs=pl.BlockSpec(memory_space=pltpu.VMEM),
        scratch_shapes=[
            pltpu.VMEM((taps_of[0], channels, channels), bf16),
            pltpu.VMEM((taps_of[1], channels, channels), bf16),
            pltpu.VMEM((blocks, rows + 2 * ROW_TILE, LANES), f32),
            pltpu.VMEM((blocks, mid_rows, LANES), f32),
            pltpu.SemaphoreType.DMA((2,)),
        ],
        compiler_params=LIMIT,
    )(first_rows, scalars, frames[0], halo, *front_pieces)

    row_pieces = [y_front]
    for bit in reversed(bits_of(shares)):
        row_pieces += [swapped(x, "tm", bit) for x in row_pieces]
    distance = [0]
    for bit in reversed(bits_of(shares)):
        distance += [d ^ bit for d in distance]
    row_pieces = [x for _, x in sorted(zip(distance, row_pieces), key=lambda pair: pair[0])]
    frame_total = rows * shares // 16

    hidden = pl.pallas_call(
        functools.partial(
            back_kernel, n_pieces, len(row_pieces), [(0, taps_of[2]), (taps_of[2], taps_of[2] + taps_of[3])]
        ),
        out_shape=jax.ShapeDtypeStruct((frame_total, LANES), bf16),
        in_specs=smem(2) + vmem(4) + unplaced(n_pieces) + vmem(len(row_pieces)),
        out_specs=pl.BlockSpec(memory_space=pltpu.VMEM),
        scratch_shapes=[
            pltpu.VMEM((taps_of[2], channels, channels), bf16),
            pltpu.VMEM((taps_of[3], channels, channels), bf16),
            pltpu.VMEM((blocks, rows * shares // 4, LANES), f32),
            pltpu.VMEM((blocks, rows * shares // 8, LANES), f32),
            pltpu.SemaphoreType.DMA((2,)),
        ],
        compiler_params=LIMIT,
    )(
        first_rows,
        scalars,
        norm_gain[None],
        norm_bias[None],
        project_weight.T,
        project_bias,
        *back_pieces,
        *row_pieces,
    )

    def partial_position(values, kind):
        return pl.pallas_call(
            functools.partial(position_kernel, len(tap_pieces)),
            out_shape=jax.ShapeDtypeStruct((frame_total, LANES), kind),
            in_specs=smem(1) + vmem(1 + len(tap_pieces)),
            out_specs=pl.BlockSpec(memory_space=pltpu.VMEM),
            scratch_shapes=[
                pltpu.VMEM((frame_total + TAPS, LANES), f32),
                pltpu.VMEM((frame_total + PHASES, own_taps * LANES), f32),
            ],
            compiler_params=LIMIT,
        )(offsets, values, *tap_pieces)

    far = stages // 2
    partner_hidden = swapped(hidden, "dp", far)
    mine = partial_position(hidden, f32)
    theirs = swapped(partial_position(partner_hidden, bf16), "dp", far)
    bias = jnp.pad(position_bias, (0, LANES - group))[None]
    encoded = pl.pallas_call(
        functools.partial(final_kernel, group),
        out_shape=jax.ShapeDtypeStruct((group, frame_total), bf16),
        in_specs=vmem(4),
        out_specs=pl.BlockSpec(memory_space=pltpu.VMEM),
    )(hidden, mine, theirs, bias)
    return encoded[None]


def solution(mesh):
    in_specs = (
        P(SHARDED, "tm", None),
        P(SHARDED),
        P(None, SHARDED, None),
        P(None, SHARDED, None),
        P(None, SHARDED, None),
        P(None, SHARDED, None),
        P(),
        P(),
        P(None, "tm"),
        P(None, "tm"),
        P("tm", SHARDED, None),
        P("tm"),
    )
    out_specs = P(SHARDED, "tm", None)
    return jax.shard_map(local, mesh=mesh, in_specs=in_specs, out_specs=out_specs, check_vma=False)
```

```python
import functools

import jax
import jax.numpy as jnp
from jax import lax
from jax.experimental import pallas as pl
from jax.experimental.pallas import tpu as pltpu
from jax.sharding import PartitionSpec as P

TAPS = 128
ROW_TILE = 16
LANES = 128
PHASES = 16
SHARDED = ("section", "dp")
eps_norm = 1e-05
f32 = jnp.float32
bf16 = jnp.bfloat16


def bits_of(size):
    return [1 << b for b in range(size.bit_length() - 1)]


def swapped(x, axis, bit):
    return lax.ppermute(x, axis, [(i, i ^ bit) for i in range(lax.axis_size(axis))])


def swapped_by_parity(x, section_bit, tm_bit, section_first):
    sections, shares = lax.axis_size("section"), lax.axis_size("tm")
    pairs = []
    for s in range(sections):
        for t in range(shares):
            over_section = (t % 2 == 0) == section_first
            to = (s ^ section_bit, t) if over_section else (s, t ^ tm_bit)
            pairs.append((s * shares + t, to[0] * shares + to[1]))
    return lax.ppermute(x, ("section", "tm"), pairs)


def flipped(where, axis, bit):
    return tuple(w ^ (bit if name == axis else 0) for w, name in zip(where, ("section", "dp", "tm"), strict=True))


def gather_weights(own, parts):
    here = (0, 0, 0)
    distances = list(range(lax.axis_size("dp")))
    received = {k: swapped(own, "dp", k) for k in reversed(distances[1:])} | {0: own}
    pieces = []
    for k in range(0, len(distances), 2):
        pair = distances[k : k + 2]
        origins = [(flipped(here, "dp", d),) * 2 for d in pair]
        pieces.append((jnp.stack([received[d] for d in pair]), origins))

    def doubled(pieces, send, even, odd):
        return [
            (jnp.concatenate([x, send(x)]), origins + [(flipped(e, *even), flipped(o, *odd)) for e, o in origins])
            for x, origins in pieces
        ]

    section_bits = bits_of(lax.axis_size("section"))
    mixed = parts == 4 and section_bits
    for bit in section_bits[: -1 if mixed else None]:
        pieces = doubled(pieces, lambda x, bit=bit: swapped(x, "section", bit), ("section", bit), ("section", bit))
    if mixed:
        bit = section_bits[-1]
        for section_first in (True, False):
            ways = (("section", bit), ("tm", 2))
            pieces = doubled(
                pieces,
                lambda x, first=section_first: swapped_by_parity(x, bit, 2, first),
                *(ways if section_first else reversed(ways)),
            )
    elif parts == 4:
        pieces = doubled(pieces, lambda x: swapped(x, "tm", 2), ("tm", 2), ("tm", 2))
    if parts >= 2:
        pieces += [
            (swapped(x, "tm", 1), [(flipped(o, "tm", 1), flipped(e, "tm", 1)) for e, o in origins]) for x, origins in pieces
        ]
    return [x for x, _ in pieces], [origin for _, origins in pieces for origin in origins]


def part_row(origin, parts, shard_rows):
    even, odd = origin
    tm = lax.axis_index("tm")
    distance = [e if e == o else jnp.where(tm % 2 == 1, o, e) for e, o in zip(even, odd, strict=True)]
    shard = (lax.axis_index("section") ^ distance[0]) * lax.axis_size("dp") + (lax.axis_index("dp") ^ distance[1])
    part = (tm % parts) ^ distance[2]
    return pl.multiple_of(shard * shard_rows + part * (shard_rows // parts), ROW_TILE)


def layer_norm(values):
    average = jnp.mean(values, axis=-1, keepdims=True)
    centred = values - average
    spread = jnp.mean(centred * centred, axis=-1, keepdims=True)
    return centred * lax.rsqrt(spread + eps_norm)


def gelu(values):
    return 0.5 * values * (1.0 + lax.erf(values * (0.5**0.5)))


def dot(a, b):
    return jnp.dot(a, b, preferred_element_type=f32)


def dot_nt(a, b):
    return lax.dot_general(a, b, (((1,), (1,)), ((), ())), preferred_element_type=f32)


def put_rows(rows_ref, start, values):
    values = values.astype(f32)
    for block in range(rows_ref.shape[0]):
        rows_ref[block, pl.ds(start, values.shape[0]), :] = values[:, block * LANES : (block + 1) * LANES]


def strided_conv(rows_ref, weight_ref, out_rows):
    summed = None
    for tap in range(weight_ref.shape[0]):
        picked = jnp.concatenate(
            [rows_ref[block, pl.ds(tap, out_rows, stride=2), :].astype(bf16) for block in range(rows_ref.shape[0])],
            axis=1,
        )
        term = dot(picked, weight_ref[tap])
        summed = term if summed is None else summed + term
    return gelu(layer_norm(summed)).astype(bf16)


def start_assembly(piece_refs, origins, parts, shard_rows, tap_slices, weight_refs, sems):
    first_rows = [part_row(origin, parts, shard_rows) for origin in origins]
    for layer, (low, high) in enumerate(tap_slices):
        part = 0
        for piece in piece_refs:
            for slot in range(piece.shape[0]):
                pltpu.make_async_copy(
                    piece.at[slot, low:high],
                    weight_refs[layer].at[:, pl.ds(first_rows[part], piece.shape[2]), :],
                    sems.at[layer],
                ).start()
                part += 1


def wait_assembly(weight_ref, sem):
    pltpu.make_async_copy(weight_ref, weight_ref, sem).wait()


def front_kernel(n_pieces, assembly, lengths, frames, halo, *rest):
    pieces, out = rest[:n_pieces], rest[n_pieces]
    w_a, w_b, x_in, x_mid, sems = rest[n_pieces + 1 :]
    start_assembly(pieces, *assembly, (w_a, w_b), sems)
    length = lengths[0]
    rows, halo_rows = frames.shape[0], halo.shape[0]
    first = lax.axis_index("tm") * rows
    channels = frames.shape[1]

    def masked(values, start):
        index = lax.broadcasted_iota(jnp.int32, (values.shape[0], 1), 0) + start
        return jnp.where(index * 20 < length, values.astype(f32), 0.0)

    put_rows(x_in, 0, masked(frames[...], first))
    put_rows(x_in, rows, masked(halo[...], first + rows))
    put_rows(x_in, rows + halo_rows, jnp.zeros((x_in.shape[1] - rows - halo_rows, channels), f32))
    wait_assembly(w_a, sems.at[0])
    put_rows(x_mid, 0, strided_conv(x_in, w_a, x_mid.shape[1]))
    wait_assembly(w_b, sems.at[1])
    out[...] = strided_conv(x_mid, w_b, out.shape[0])


def back_kernel(n_pieces, n_rows, assembly, lengths, gain, bias, project, project_bias, *rest):
    pieces, row_pieces, out = rest[:n_pieces], rest[n_pieces : n_pieces + n_rows], rest[n_pieces + n_rows]
    w_a, w_b, x_in, x_mid, sems = rest[n_pieces + n_rows + 1 :]
    start_assembly(pieces, *assembly, (w_a, w_b), sems)
    length, tm = lengths[0], lax.axis_index("tm")
    for index, piece in enumerate(row_pieces):
        rows = piece.shape[0]
        put_rows(x_in, pl.multiple_of((tm ^ index) * rows, ROW_TILE), piece[...])
    wait_assembly(w_a, sems.at[0])
    put_rows(x_mid, 0, strided_conv(x_in, w_a, x_mid.shape[1]))
    wait_assembly(w_b, sems.at[1])
    frames, group = out.shape[0], project.shape[0]
    extracted = strided_conv(x_mid, w_b, frames).astype(f32)
    normed = (layer_norm(extracted) * gain[...] + bias[...]).astype(bf16)
    hidden = (dot_nt(normed, project[...]) + project_bias[...].astype(f32)).astype(bf16)
    index = lax.broadcasted_iota(jnp.int32, (frames, 1), 0)
    hidden = jnp.where(index * 320 < length, hidden.astype(f32), 0.0)
    out[...] = jnp.zeros(out.shape, bf16)
    out[:, 0:group] = hidden.astype(bf16)


def position_kernel(n_pieces, places, hidden, *rest):
    pieces, out, padded, phases = rest[:n_pieces], rest[n_pieces], rest[n_pieces + 1], rest[n_pieces + 2]
    frames = hidden.shape[0]
    padded[...] = jnp.zeros(padded.shape, f32)
    padded[TAPS // 2 : TAPS // 2 + frames, :] = hidden[...].astype(f32)
    taps, width = pieces[0].shape[0], pieces[0].shape[1]
    span = phases.shape[0]
    for index, piece in enumerate(pieces):
        shard = (lax.axis_index("section") ^ places[index][0]) * lax.axis_size("dp")
        shard += lax.axis_index("dp") ^ places[index][1]
        window = padded[pl.ds(shard * taps, span), :].astype(bf16)
        term = dot_nt(window, piece[...].reshape(taps * width, piece.shape[2]))
        if index == 0:
            phases[...] = term
        else:
            phases[...] += term
    total = phases[0:frames, 0:width]
    for tap in range(1, taps):
        total = total + phases[tap : tap + frames, tap * width : (tap + 1) * width]
    out[...] = total.astype(out.dtype)


def final_kernel(group, hidden, mine, theirs, bias, out):
    conv = mine[...] + theirs[...].astype(f32)
    encoded = hidden[...].astype(f32) + gelu(conv + bias[...])
    out[...] = jnp.transpose(encoded)[0:group, :].astype(bf16)


def layer_taps(counts):
    return [(sum(counts[:i]), sum(counts[: i + 1])) for i in range(len(counts))]


def vmem(count):
    return [pl.BlockSpec(memory_space=pltpu.VMEM)] * count


def smem(count):
    return [pl.BlockSpec(memory_space=pltpu.SMEM)] * count


def unplaced(count):
    return [pl.BlockSpec(memory_space=pl.ANY)] * count


LIMIT = pltpu.CompilerParams(vmem_limit_bytes=16 * 1024 * 1024)


def local(
    frames,
    lengths,
    fourth_conv,
    fifth_conv,
    sixth_conv,
    seventh_conv,
    norm_gain,
    norm_bias,
    project_weight,
    project_bias,
    position_weight,
    position_bias,
):
    sections, stages, shares = (lax.axis_size(a) for a in ("section", "dp", "tm"))
    tm = lax.axis_index("tm")
    rows, channels = frames.shape[1:]
    shard_rows = fourth_conv.shape[1]
    parts = max(p for p in (1, 2, 4) if p <= shares and shard_rows % (p * ROW_TILE) == 0)
    part_rows = shard_rows // parts
    part = tm % parts

    def own_part(weights):
        return jnp.concatenate(
            [lax.dynamic_slice_in_dim(w, part * part_rows, part_rows, 1) for w in weights], axis=0
        )

    halo = lax.ppermute(frames[0, :ROW_TILE], "tm", [(i + 1, i) for i in range(shares - 1)])
    front_pieces, origins = gather_weights(own_part([fourth_conv, fifth_conv]), parts)
    back_own, front_pieces[0] = lax.optimization_barrier((own_part([sixth_conv, seventh_conv]), front_pieces[0]))
    back_pieces, _ = gather_weights(back_own, parts)

    group = position_bias.shape[0]
    own_taps = position_weight.shape[1]
    taps = position_weight[0].reshape(own_taps, group, group)
    taps = jnp.pad(taps, ((0, 0), (0, LANES - group), (0, LANES - group)))
    tap_pieces, tap_places = [taps], [(0, 0, 0)]
    for axis, bits in (("section", bits_of(sections)), ("dp", bits_of(stages)[:-1])):
        for bit in bits:
            tap_pieces += [swapped(x, axis, bit) for x in tap_pieces]
            tap_places += [flipped(p, axis, bit) for p in tap_places]
    taps_of = [w.shape[0] for w in (fourth_conv, fifth_conv, sixth_conv, seventh_conv)]
    n_pieces = len(front_pieces)
    blocks = channels // LANES
    mid_rows = (rows // 2 + 8) // 8 * 8
    y_front = pl.pallas_call(
        functools.partial(front_kernel, n_pieces, (origins, parts, shard_rows, layer_taps(taps_of[:2]))),
        out_shape=jax.ShapeDtypeStruct((rows // 4, channels), bf16),
        in_specs=smem(1) + vmem(2) + unplaced(n_pieces),
        out_specs=pl.BlockSpec(memory_space=pltpu.VMEM),
        scratch_shapes=[
            pltpu.VMEM((taps_of[0], channels, channels), bf16),
            pltpu.VMEM((taps_of[1], channels, channels), bf16),
            pltpu.VMEM((blocks, rows + 2 * ROW_TILE, LANES), f32),
            pltpu.VMEM((blocks, mid_rows, LANES), f32),
            pltpu.SemaphoreType.DMA((2,)),
        ],
        compiler_params=LIMIT,
    )(lengths, frames[0], halo, *front_pieces)

    row_pieces = [y_front]
    for bit in reversed(bits_of(shares)):
        row_pieces += [swapped(x, "tm", bit) for x in row_pieces]
    distance = [0]
    for bit in reversed(bits_of(shares)):
        distance += [d ^ bit for d in distance]
    row_pieces = [x for _, x in sorted(zip(distance, row_pieces), key=lambda pair: pair[0])]
    frame_total = rows * shares // 16

    hidden = pl.pallas_call(
        functools.partial(
            back_kernel, n_pieces, len(row_pieces), (origins, parts, shard_rows, layer_taps(taps_of[2:]))
        ),
        out_shape=jax.ShapeDtypeStruct((frame_total, LANES), bf16),
        in_specs=smem(1) + vmem(4) + unplaced(n_pieces) + vmem(len(row_pieces)),
        out_specs=pl.BlockSpec(memory_space=pltpu.VMEM),
        scratch_shapes=[
            pltpu.VMEM((taps_of[2], channels, channels), bf16),
            pltpu.VMEM((taps_of[3], channels, channels), bf16),
            pltpu.VMEM((blocks, rows * shares // 4, LANES), f32),
            pltpu.VMEM((blocks, rows * shares // 8, LANES), f32),
            pltpu.SemaphoreType.DMA((2,)),
        ],
        compiler_params=LIMIT,
    )(
        lengths,
        norm_gain[None],
        norm_bias[None],
        project_weight.T,
        project_bias,
        *back_pieces,
        *row_pieces,
    )

    def partial_position(values, kind):
        return pl.pallas_call(
            functools.partial(position_kernel, len(tap_pieces), tap_places),
            out_shape=jax.ShapeDtypeStruct((frame_total, LANES), kind),
            in_specs=vmem(1 + len(tap_pieces)),
            out_specs=pl.BlockSpec(memory_space=pltpu.VMEM),
            scratch_shapes=[
                pltpu.VMEM((frame_total + TAPS, LANES), f32),
                pltpu.VMEM((frame_total + PHASES, own_taps * LANES), f32),
            ],
            compiler_params=LIMIT,
        )(values, *tap_pieces)

    far = stages // 2
    partner_hidden = swapped(hidden, "dp", far)
    mine = partial_position(hidden, f32)
    theirs = swapped(partial_position(partner_hidden, bf16), "dp", far)
    bias = jnp.pad(position_bias, (0, LANES - group))[None]
    encoded = pl.pallas_call(
        functools.partial(final_kernel, group),
        out_shape=jax.ShapeDtypeStruct((group, frame_total), bf16),
        in_specs=vmem(4),
        out_specs=pl.BlockSpec(memory_space=pltpu.VMEM),
    )(hidden, mine, theirs, bias)
    return encoded[None]


def solution(mesh):
    in_specs = (
        P(SHARDED, "tm", None),
        P(SHARDED),
        P(None, SHARDED, None),
        P(None, SHARDED, None),
        P(None, SHARDED, None),
        P(None, SHARDED, None),
        P(),
        P(),
        P(None, "tm"),
        P(None, "tm"),
        P("tm", SHARDED, None),
        P("tm"),
    )
    out_specs = P(SHARDED, "tm", None)
    return jax.shard_map(local, mesh=mesh, in_specs=in_specs, out_specs=out_specs, check_vma=False)
```

```python
import functools

import jax
import jax.numpy as jnp
from jax import lax
from jax.experimental import pallas as pl
from jax.experimental.pallas import tpu as pltpu
from jax.sharding import PartitionSpec as P

TAPS = 128
ROW_TILE = 16
LANES = 128
PHASES = 16
SHARDED = ("section", "dp")
eps_norm = 1e-05
f32 = jnp.float32
bf16 = jnp.bfloat16


def bits_of(size):
    return [1 << b for b in range(size.bit_length() - 1)]


def swapped(x, axis, bit):
    return lax.ppermute(x, axis, [(i, i ^ bit) for i in range(lax.axis_size(axis))])


def swapped_by_parity(x, section_bit, tm_bit, section_first):
    sections, shares = lax.axis_size("section"), lax.axis_size("tm")
    pairs = []
    for s in range(sections):
        for t in range(shares):
            over_section = (t % 2 == 0) == section_first
            to = (s ^ section_bit, t) if over_section else (s, t ^ tm_bit)
            pairs.append((s * shares + t, to[0] * shares + to[1]))
    return lax.ppermute(x, ("section", "tm"), pairs)


def flipped(where, axis, bit):
    return tuple(w ^ (bit if name == axis else 0) for w, name in zip(where, ("section", "dp", "tm"), strict=True))


def after(x, *others):
    return lax.optimization_barrier((x, *others))[0]


def paired(received):
    odd = lax.axis_index("dp") % 2 == 1
    pieces = []
    for first in range(0, len(received), 2):
        one, other = received[first : first + 2]
        pair = jnp.where(odd, jnp.stack([other, one]), jnp.stack([one, other]))
        pieces.append((pair, [((0, first, 0),) * 2]))
    return pieces


def gated(pieces, *others):
    return pieces[:-1] + [(after(pieces[-1][0], *others), pieces[-1][1])]


def wide_steps(parts):
    bits = bits_of(lax.axis_size("section"))
    mixed = parts == 4 and len(bits) > 0
    steps = []
    for bit in bits[: -1 if mixed else None]:
        steps.append((lambda x, bit=bit: swapped(x, "section", bit), ("section", bit), ("section", bit)))
    if mixed:
        ways = (("section", bits[-1]), ("tm", 2))
        steps.append((lambda x: swapped_by_parity(x, bits[-1], 2, True), *ways))
        steps.append((lambda x: swapped_by_parity(x, bits[-1], 2, False), *reversed(ways)))
    elif parts == 4:
        steps.append((lambda x: swapped(x, "tm", 2), ("tm", 2), ("tm", 2)))
    return steps


def doubled(pieces, step):
    send, even, odd = step
    return [
        (jnp.concatenate([x, send(x)]), origins + [(flipped(e, *even), flipped(o, *odd)) for e, o in origins])
        for x, origins in pieces
    ]


def sent(piece, step):
    (x, origins), (send, even, odd) = piece, step
    return send(x), [(flipped(e, *even), flipped(o, *odd)) for e, o in origins]


def joined(*pieces):
    return jnp.concatenate([x for x, _ in pieces]), [origin for _, origins in pieces for origin in origins]


def with_cores(pieces, parts):
    if parts >= 2:
        pieces = pieces + [
            (swapped(x, "tm", 1), [(flipped(o, "tm", 1), flipped(e, "tm", 1)) for e, o in origins]) for x, origins in pieces
        ]
    return [x for x, _ in pieces], [origin for _, origins in pieces for origin in origins]


def layer_norm(values):
    average = jnp.mean(values, axis=-1, keepdims=True)
    centred = values - average
    spread = jnp.mean(centred * centred, axis=-1, keepdims=True)
    return centred * lax.rsqrt(spread + eps_norm)


def gelu(values):
    return 0.5 * values * (1.0 + lax.erf(values * (0.5**0.5)))


def dot(a, b):
    return jnp.dot(a, b, preferred_element_type=f32)


def dot_nt(a, b):
    return lax.dot_general(a, b, (((1,), (1,)), ((), ())), preferred_element_type=f32)


def put_rows(rows_ref, start, values):
    values = values.astype(f32)
    for block in range(rows_ref.shape[0]):
        rows_ref[block, pl.ds(start, values.shape[0]), :] = values[:, block * LANES : (block + 1) * LANES]


def strided_conv(rows_ref, weights_ref, taps, out_rows):
    channels = weights_ref.shape[3]
    summed = None
    for tap in range(taps[1] - taps[0]):
        picked = jnp.concatenate(
            [rows_ref[block, pl.ds(tap, out_rows, stride=2), :].astype(bf16) for block in range(rows_ref.shape[0])],
            axis=1,
        )
        term = dot(picked, weights_ref[:, taps[0] + tap].reshape(channels, channels))
        summed = term if summed is None else summed + term
    return gelu(layer_norm(summed)).astype(bf16)


def start_assembly(piece_refs, origins, weights_ref, sem):
    tm, stages = lax.axis_index("tm"), lax.axis_size("dp")
    parts = weights_ref.shape[2] // piece_refs[0].shape[2]
    slots = ((piece, first) for piece in piece_refs for first in range(0, piece.shape[0], 2))
    for (piece, first), (even, odd) in zip(slots, origins, strict=True):
        distance = [e if e == o else jnp.where(tm % 2 == 1, o, e) for e, o in zip(even, odd, strict=True)]
        shard = (lax.axis_index("section") ^ distance[0]) * stages + (lax.axis_index("dp") ^ distance[1]) // 2 * 2
        rows = piece.shape[2]
        row = pl.multiple_of(((tm % parts) ^ distance[2]) * rows, ROW_TILE)
        pltpu.make_async_copy(
            piece.at[first : first + 2], weights_ref.at[pl.ds(shard, 2), :, pl.ds(row, rows), :], sem
        ).start()


def own_part_kernel(parts, *refs):
    weights, out, sems = refs[:-2], refs[-2], refs[-1]
    rows = out.shape[1]
    row = pl.multiple_of(lax.axis_index("tm") % parts * rows, ROW_TILE)
    copies = []
    for index, (low, high) in enumerate(taps_between([w.shape[0] for w in weights])):
        source = weights[index].at[:, pl.ds(row, rows), :]
        copies.append(pltpu.make_async_copy(source, out.at[low:high], sems.at[index]))
    for copy in copies:
        copy.start()
    for copy in copies:
        copy.wait()


def layers_kernel(n_pieces, origins, layer_taps, lengths, frames, halo, gain, bias, *rest):
    pieces, out = rest[:n_pieces], rest[n_pieces]
    weights, gain_here, bias_here, *inputs, sem, small_sems = rest[n_pieces + 1 :]
    start_assembly(pieces, origins, weights, sem)
    small = [
        pltpu.make_async_copy(gain, gain_here, small_sems.at[0]),
        pltpu.make_async_copy(bias, bias_here, small_sems.at[1]),
    ]
    for copy in small:
        copy.start()
    length = lengths[0]
    rows, halo_rows = frames.shape[0], halo.shape[0]
    first = lax.axis_index("tm") * rows
    channels = frames.shape[1]

    def masked(values, start):
        index = lax.broadcasted_iota(jnp.int32, (values.shape[0], 1), 0) + start
        return jnp.where(index * 20 < length, values.astype(f32), 0.0)

    x_in = inputs[0]
    put_rows(x_in, 0, masked(frames[...], first))
    put_rows(x_in, rows, masked(halo[...], first + rows))
    put_rows(x_in, rows + halo_rows, jnp.zeros((x_in.shape[1] - rows - halo_rows, channels), f32))
    pltpu.make_async_copy(weights, weights, sem).wait()
    for layer, taps in enumerate(layer_taps[:-1]):
        following = inputs[layer + 1]
        put_rows(following, 0, strided_conv(inputs[layer], weights, taps, following.shape[1]))
    extracted = strided_conv(inputs[-1], weights, layer_taps[-1], out.shape[0]).astype(f32)
    for copy in small:
        copy.wait()
    out[...] = (layer_norm(extracted) * gain_here[...] + bias_here[...]).astype(bf16)


def project_kernel(lengths, project, project_bias, *rest):
    pieces, out, rows_ref = rest[:-2], rest[-2], rest[-1]
    tm = lax.axis_index("tm")
    for index, piece in enumerate(pieces):
        rows = piece.shape[0]
        rows_ref[pl.ds(pl.multiple_of((tm ^ index) * rows, ROW_TILE), rows), :] = piece[...]
    frames, group = out.shape[0], project.shape[0]
    hidden = (dot_nt(rows_ref[...], project[...]) + project_bias[...].astype(f32)).astype(bf16)
    index = lax.broadcasted_iota(jnp.int32, (frames, 1), 0)
    hidden = jnp.where(index * 320 < lengths[0], hidden.astype(f32), 0.0)
    out[...] = jnp.zeros(out.shape, bf16)
    out[:, 0:group] = hidden.astype(bf16)


def position_kernel(n_pieces, own_taps, places, hidden, *rest):
    pieces, out, padded, phases = rest[:n_pieces], rest[n_pieces], rest[n_pieces + 1], rest[n_pieces + 2]
    frames = hidden.shape[0]
    padded[...] = jnp.zeros(padded.shape, f32)
    padded[TAPS // 2 : TAPS // 2 + frames, :] = hidden[...].astype(f32)
    taps, width = pieces[0].shape[0:2]
    span = phases.shape[0]
    for index, piece in enumerate(pieces):
        place, first_tap = places[index]
        shard = (lax.axis_index("section") ^ place[0]) * lax.axis_size("dp") + (lax.axis_index("dp") ^ place[1])
        window = padded[pl.ds(shard * own_taps + first_tap, span), :].astype(bf16)
        term = dot_nt(window, piece[...].reshape(taps * width, piece.shape[2]))
        if index == 0:
            phases[...] = term
        else:
            phases[...] += term
    total = phases[0:frames, 0:width]
    for tap in range(1, taps):
        total = total + phases[tap : tap + frames, tap * width : (tap + 1) * width]
    out[...] = total.astype(out.dtype)


def final_kernel(hidden, mine, theirs, bias, out):
    group = out.shape[0]
    conv = mine[...] + theirs[...].astype(f32)
    position = gelu(conv[:, 0:group] + bias[...])
    out[...] = jnp.transpose(hidden[:, 0:group].astype(f32) + position).astype(bf16)


def taps_between(counts):
    return [(sum(counts[:i]), sum(counts[: i + 1])) for i in range(len(counts))]


def vmem(count):
    return [pl.BlockSpec(memory_space=pltpu.VMEM)] * count


def smem(count):
    return [pl.BlockSpec(memory_space=pltpu.SMEM)] * count


def unplaced(count):
    return [pl.BlockSpec(memory_space=pl.ANY)] * count


LIMIT = pltpu.CompilerParams(vmem_limit_bytes=12 * 1024 * 1024)


def local(
    frames,
    lengths,
    fourth_conv,
    fifth_conv,
    sixth_conv,
    seventh_conv,
    norm_gain,
    norm_bias,
    project_weight,
    project_bias,
    position_weight,
    position_bias,
):
    sections, stages, shares = (lax.axis_size(a) for a in ("section", "dp", "tm"))
    tm = lax.axis_index("tm")
    rows, channels = frames.shape[1:]
    shard_rows = fourth_conv.shape[1]
    parts = max(p for p in (1, 2, 4) if p <= shares and shard_rows % (p * ROW_TILE) == 0)
    part_rows = shard_rows // parts

    group = position_bias.shape[0]
    own_taps = position_weight.shape[1]
    flat_taps, tap_places = [position_weight], [(0, 0, 0)]
    for bit in bits_of(sections):
        flat_taps += [swapped(x, "section", bit) for x in flat_taps]
        tap_places += [flipped(p, "section", bit) for p in tap_places]

    convs = (fourth_conv, fifth_conv, sixth_conv, seventh_conv)
    taps_of = [w.shape[0] for w in convs]
    own = pl.pallas_call(
        functools.partial(own_part_kernel, parts),
        out_shape=jax.ShapeDtypeStruct((sum(taps_of), part_rows, channels), bf16),
        in_specs=unplaced(len(convs)),
        out_specs=pl.BlockSpec(memory_space=pltpu.VMEM),
        scratch_shapes=[pltpu.SemaphoreType.DMA((len(convs),))],
    )(*convs)
    *first, last = paired([own] + [swapped(own, "dp", d) for d in range(1, stages)])
    last = [last]

    def tap_matrices(flat):
        square = flat.reshape(own_taps, group, group)
        return jnp.pad(square, ((0, 0), (0, LANES - group), (0, LANES - group)))

    tap_block = max(own_taps // 2, 1)
    tap_pieces = []
    for flat, place in zip(flat_taps, tap_places, strict=True):
        matrices = tap_matrices(flat)
        tap_pieces += [(matrices[k : k + tap_block], place, k) for k in range(0, own_taps, tap_block)]
    near_count = len(tap_pieces)
    near_taps = [x for x, _, _ in tap_pieces]
    for bit in bits_of(stages)[:-1]:
        tap_pieces += [(swapped(x, "dp", bit), flipped(p, "dp", bit), k) for x, p, k in tap_pieces]
    far_taps = [x for x, _, _ in tap_pieces[near_count:]]
    quarter = -(-len(far_taps) // 4)
    far_quarters = [far_taps[k * quarter : (k + 1) * quarter] for k in range(4)]

    rim = frames[0, :ROW_TILE]
    from_even = lax.ppermute(after(rim, last[0][0], *far_quarters[0]), "tm", [(i, i ^ 1) for i in range(shares)])
    from_odd = lax.ppermute(rim, "tm", [(i, (i + 1 if i % 2 else i - 1) % shares) for i in range(shares)])
    halo = jnp.where(tm % 2 == 0, from_even, jnp.where(tm == shares - 1, jnp.zeros_like(rim), from_odd))

    steps = wide_steps(parts)
    if len(steps) == 2:
        (m1,), (m2,) = first, last
        n1 = sent(m1, steps[0])
        q1 = sent((after(m1[0], *near_taps), m1[1]), steps[1])
        both = joined(n1, m2)
        both = sent((after(both[0], q1[0], from_even), both[1]), steps[1])
        n2 = (both[0][-m2[0].shape[0] :], both[1][-len(m2[1]) :])
        rest = joined(m2, n2)
        rest = sent((after(rest[0], halo, *far_quarters[1]), rest[1]), steps[0])
        pieces = [joined(m1, n1, q1, m2), both, (after(rest[0], *far_quarters[2]), rest[1])]
    else:
        pieces = first + last
        for step in steps:
            pieces = doubled(pieces, step)
    pieces, origins = with_cores(pieces, parts)

    blocks = channels // LANES
    row_counts = [rows + 2 * ROW_TILE, (rows // 2 + 8) // 8 * 8, rows // 4, rows // 8]
    normed = pl.pallas_call(
        functools.partial(layers_kernel, len(pieces), origins, taps_between(taps_of)),
        out_shape=jax.ShapeDtypeStruct((rows // 16, channels), bf16),
        in_specs=smem(1) + vmem(2) + unplaced(2 + len(pieces)),
        out_specs=pl.BlockSpec(memory_space=pltpu.VMEM),
        scratch_shapes=[
            pltpu.VMEM((sections * stages, sum(taps_of), shard_rows, channels), bf16),
            pltpu.VMEM((1, channels), f32),
            pltpu.VMEM((1, channels), f32),
            *(pltpu.VMEM((blocks, count, LANES), f32) for count in row_counts),
            pltpu.SemaphoreType.DMA(()),
            pltpu.SemaphoreType.DMA((2,)),
        ],
        compiler_params=LIMIT,
    )(lengths, frames[0], halo, norm_gain[None], norm_bias[None], *pieces)

    row_pieces = [normed]
    for bit in reversed(bits_of(shares)):
        if bit == 1:
            row_pieces[-1] = after(row_pieces[-1], *far_quarters[3])
        row_pieces += [swapped(x, "tm", bit) for x in row_pieces]
    distance = [0]
    for bit in reversed(bits_of(shares)):
        distance += [d ^ bit for d in distance]
    row_pieces = [x for _, x in sorted(zip(distance, row_pieces), key=lambda pair: pair[0])]
    frame_total = rows * shares // 16

    hidden = pl.pallas_call(
        project_kernel,
        out_shape=jax.ShapeDtypeStruct((frame_total, LANES), bf16),
        in_specs=smem(1) + vmem(2 + len(row_pieces)),
        out_specs=pl.BlockSpec(memory_space=pltpu.VMEM),
        scratch_shapes=[pltpu.VMEM((frame_total, channels), bf16)],
        compiler_params=LIMIT,
    )(lengths, project_weight.T, project_bias, *row_pieces)

    def partial_position(values, kind):
        return pl.pallas_call(
            functools.partial(position_kernel, len(tap_pieces), own_taps, [(p, k) for _, p, k in tap_pieces]),
            out_shape=jax.ShapeDtypeStruct((frame_total, LANES), kind),
            in_specs=vmem(1 + len(tap_pieces)),
            out_specs=pl.BlockSpec(memory_space=pltpu.VMEM),
            scratch_shapes=[
                pltpu.VMEM((frame_total + TAPS + PHASES, LANES), f32),
                pltpu.VMEM((frame_total + PHASES, tap_block * LANES), f32),
            ],
            compiler_params=LIMIT,
        )(values, *(x for x, _, _ in tap_pieces))

    far = stages // 2
    partner_hidden = swapped(hidden, "dp", far)
    mine = partial_position(hidden, f32)
    theirs = swapped(partial_position(after(partner_hidden, mine), bf16), "dp", far)
    encoded = pl.pallas_call(
        final_kernel,
        out_shape=jax.ShapeDtypeStruct((group, frame_total), bf16),
        in_specs=vmem(4),
        out_specs=pl.BlockSpec(memory_space=pltpu.VMEM),
        compiler_params=LIMIT,
    )(hidden, mine, theirs, position_bias[None])
    return encoded[None]


def solution(mesh):
    in_specs = (
        P(SHARDED, "tm", None),
        P(SHARDED),
        P(None, SHARDED, None),
        P(None, SHARDED, None),
        P(None, SHARDED, None),
        P(None, SHARDED, None),
        P(),
        P(),
        P(None, "tm"),
        P(None, "tm"),
        P("tm", SHARDED, None),
        P("tm"),
    )
    out_specs = P(SHARDED, "tm", None)
    return jax.shard_map(local, mesh=mesh, in_specs=in_specs, out_specs=out_specs, check_vma=False)
```
